128 devices in a mesh: row: 16 (over z, y_lo, core), col: 8 (over y_hi, x).
Axes of the slice: x: 4, y: 4 (y_hi: 2, y_lo: 2; y = y_hi * 2 + y_lo), z: 4, core: 2. Of those that a mesh axis runs over, the one named last changes fastest.
Arguments:
- gram_x: float32 [8192, 8192], P('row', 'col'), may hold values from -0.44194174 to 0.44194174, as said below
- cross: float32 [8192, 8192], P('row', 'col'), may hold values from -0.0625 to 0.0625
- gram_y: float32 [8192, 8192], P('row', 'col'), may hold values from -0.44194174 to 0.44194174, as said below
- shifts: float32 [4], replicated, may hold values from -1.5 to 1.5
- modes: bfloat16 [2048, 8192], P('row', 'col'), may hold values from -6 to 6
Outputs:
- products: float32 [4, 2048, 8192], P(None, 'row', 'col')
The draws below stay inside these ranges and needn't reach their ends.
Inputs may be any that keep to these rules, and one draw needn't show every extreme that they name: `gram_x`: exactly symmetric. `gram_y`: exactly symmetric.
All inputs are finite; a program needn't handle non-finite values.
Results may differ from the reference program's by a relative error of at most 0.0029.
Values may be sent and summed in bfloat16 or wider, within the bound.
No kernel may reach another device: no remote copies, remote signals or barrier semaphores. Data moves between devices by JAX's collectives and lax.ppermute only.
A program may use at most 192 MiB of HBM per device.

```python
import jax
import jax.numpy as jnp
from jax import lax

DICT = 8192
SHIFTS = 4
MODES = 2048


def symmetric_matrix(key):
    base = jax.random.truncated_normal(key, -4.0, 4.0, (DICT, DICT), jnp.float32)
    base = base * DICT ** (-0.5)
    return (base + base.T) * 0.5


def draw_gram_x(key, part):
    key = jax.random.fold_in(key, 11)
    return symmetric_matrix(key)


def draw_gram_y(key, part):
    key = jax.random.fold_in(key, 23)
    return symmetric_matrix(key)


def block_scale(rng, extent, split, least, high):
    def one(dim, parts):
        draws = jax.random.uniform(jax.random.fold_in(jax.random.fold_in(rng, 6), dim), (parts,), jnp.float32, least / len(split), high / len(split))
        return jnp.repeat(jnp.exp(draws), extent[dim] // parts).reshape((-1,) + (1,) * (len(extent) - dim - 1))

    level = one(*split[0])
    for cut in split[1:]:
        level = level * one(*cut)
    return level


def bell_draw(own_key, dims, deviation, reach, cuts=(), held_as=jnp.bfloat16):
    entries = jax.random.normal(own_key, dims, jnp.float32) * deviation
    if len(cuts) > 0:
        entries = block_scale(own_key, dims, cuts, -0.22, 0.18) * entries
    return jnp.clip(entries, min=-reach, max=reach).astype(held_as)


def setup_inputs(seed: int = 0) -> dict:
    key_list = jax.random.split(jax.random.key(seed), 6)
    gram_x = draw_gram_x(jax.random.fold_in(key_list[5], 71), 0)
    cross = bell_draw(key_list[1], (DICT, DICT), DICT ** -0.5, 0.0625, ((0, 16), (1, 8)), jnp.float32)
    gram_y = draw_gram_y(jax.random.fold_in(key_list[5], 71), 0)
    shifts = jnp.clip(jax.random.uniform(key_list[3], (SHIFTS,), jnp.float32, -1.5, 1.5), -1.5, 1.5)
    modes = bell_draw(key_list[4], (MODES, DICT), 1.0, 6.0, ((0, 16), (1, 8)))
    return {"gram_x": gram_x, "cross": cross, "gram_y": gram_y, "shifts": shifts, "modes": modes}


def reference(gram_x, cross, gram_y, shifts, modes):
    low_x = gram_x.astype(jnp.bfloat16)
    low_a = cross.astype(jnp.bfloat16)
    low_y = gram_y.astype(jnp.bfloat16)
    from_gram_y = jnp.dot(modes, low_y, preferred_element_type=jnp.float32)
    from_gram_x = jnp.dot(modes, low_x, preferred_element_type=jnp.float32)
    from_cross_t = jnp.dot(modes, low_a, preferred_element_type=jnp.float32)
    from_cross = lax.dot_general(modes, low_a, (((1,), (1,)), ((), ())), preferred_element_type=jnp.float32)
    shift_col = shifts[:, None, None]
    return from_gram_y[None] - shift_col * (from_cross + from_cross_t)[None] + shift_col * shift_col * from_gram_x[None]
```

```python
import jax
import jax.numpy as jnp
from jax import lax
from jax.experimental import pallas as pl
from jax.experimental.pallas import tpu as pltpu
from jax.sharding import PartitionSpec as P

BOTH = ("row", "col")
BF16 = jnp.bfloat16
F32 = jnp.float32
VMEM_BYTES = 48 * 2**20


def moves(n_row, n_col, target):
    pairs = []
    for block in range(n_row // 2):
        for core in range(2):
            for col in range(n_col):
                to_block, to_core, to_col = target(block, core, col)
                pairs.append(((2 * block + core) * n_col + col, (2 * to_block + to_core) * n_col + to_col))
    return pairs


def after(array, *others):
    return lax.optimization_barrier((array,) + others)[0]


def call(body, place, grid, in_specs, out_spec, out_shape, scratch, flops, *args):
    return pl.pallas_call(
        body,
        grid_spec=pltpu.PrefetchScalarGridSpec(
            num_scalar_prefetch=1, grid=grid, in_specs=in_specs, out_specs=out_spec, scratch_shapes=scratch
        ),
        out_shape=out_shape,
        compiler_params=pltpu.CompilerParams(vmem_limit_bytes=VMEM_BYTES),
        cost_estimate=pl.CostEstimate(
            flops=flops,
            bytes_accessed=sum(a.size * a.dtype.itemsize for a in args) + out_shape.size * 2,
            transcendentals=0,
        ),
    )(place, *args)


def untransposed(part, mine, other, place):
    slots, modes, depth = part.shape
    half, width = mine.shape
    block = 512

    def body(place, part, mine, other, out, tile):
        tile[pl.ds(pl.multiple_of(place[0] * half, half), half)] = mine[...].astype(BF16)
        tile[pl.ds(pl.multiple_of((1 - place[0]) * half, half), half)] = other[...].astype(BF16)
        rows = part[...].reshape(slots * modes, depth)
        total = jnp.dot(rows, tile[...], preferred_element_type=F32).astype(BF16)
        for slot in range(slots):
            out[place[1 + slot]] = total[slot * modes : (slot + 1) * modes]

    return call(
        body,
        place,
        (width // block,),
        [
            pl.BlockSpec((slots, modes, depth), lambda n, place: (0, 0, 0)),
            pl.BlockSpec((half, block), lambda n, place: (0, n)),
            pl.BlockSpec((half, block), lambda n, place: (0, n)),
        ],
        pl.BlockSpec((slots, modes, block), lambda n, place: (0, 0, n)),
        jax.ShapeDtypeStruct((slots, modes, width), BF16),
        [pltpu.VMEM((2 * half, block), BF16)],
        2 * slots * modes * depth * width,
        part,
        mine,
        other,
    )


def transposed(part, mine, other, place):
    slots, modes, depth = part.shape
    half = mine.shape[0]
    block = 512
    blocks = half // block

    def body(place, part, mine, other, out):
        own = pl.program_id(0) // blocks == place[0]
        tile = jnp.where(own, mine[...], other[...]).astype(BF16)
        rows = part[...].reshape(slots * modes, depth)
        total = lax.dot_general(rows, tile, (((1,), (1,)), ((), ())), preferred_element_type=F32)
        total = total.astype(BF16)
        for slot in range(slots):
            out[place[1 + slot]] = total[slot * modes : (slot + 1) * modes]

    return call(
        body,
        place,
        (2 * blocks,),
        [
            pl.BlockSpec((slots, modes, depth), lambda n, place: (0, 0, 0)),
            pl.BlockSpec((block, depth), lambda n, place: (n % blocks, 0)),
            pl.BlockSpec((block, depth), lambda n, place: (n % blocks, 0)),
        ],
        pl.BlockSpec((slots, modes, block), lambda n, place: (0, 0, n)),
        jax.ShapeDtypeStruct((slots, modes, 2 * half), BF16),
        [],
        4 * slots * modes * depth * half,
        part,
        mine,
        other,
    )


def shards(n_row, n_col, gram_x, cross, gram_y, shifts, modes):
    row, col = lax.axis_index("row"), lax.axis_index("col")
    core, block = row % 2, row // 2
    n_block = n_row // 2
    ring = n_col // 2
    swap_cores = moves(n_row, n_col, lambda block, core, col: (block, 1 - core, col))

    turned = lax.ppermute(
        modes, BOTH, moves(n_row, n_col, lambda block, core, col: (col, core, block ^ col))
    )
    pair = lax.ppermute(modes, BOTH, moves(n_row, n_col, lambda block, core, col: (block ^ 1, core, col)))
    gram_x_pair, cross_pair, gram_y_pair = [
        (tile, lax.ppermute(tile, BOTH, swap_cores)) for tile in (gram_x, cross, gram_y)
    ]
    pair = after(jnp.stack((modes, pair)), gram_x_pair, cross_pair, gram_y_pair)
    stripe = [pair]
    for step in range(2, n_block, 2):
        pairs = moves(n_row, n_col, lambda block, core, col: (block ^ step, core, col))
        stripe.append(lax.ppermute(pair, BOTH, pairs))

    copies = jnp.broadcast_to(after(turned, pair)[None], (n_col,) + turned.shape)
    swath = lax.all_to_all(copies, "col", split_axis=0, concat_axis=0, tiled=True)

    stripe = jnp.concatenate(stripe, axis=0)
    def start(product, ahead, back):
        parts = product.reshape((4, 2, -1) + product.shape[2:])
        return parts, lax.ppermute(parts[2, 0], BOTH, ahead), lax.ppermute(parts[2, 1], BOTH, back)

    def join(parts, came_ahead, came_back):
        def plus(part, came):
            return (part.astype(F32) + came.astype(F32)).astype(BF16)

        return (
            parts[0],
            jnp.stack((plus(parts[1, 0], came_ahead), parts[1, 1])),
            jnp.stack((parts[3, 0], plus(parts[3, 1], came_back))),
        )

    def finish(parts, ahead, back):
        mine, on, off = parts
        return (
            mine.astype(F32)
            + lax.ppermute(on, BOTH, ahead).astype(F32)
            + lax.ppermute(off, BOTH, back).astype(F32)
        )

    def fold(total, partner, dtype):
        return total[0] + lax.ppermute(total[1].astype(dtype), BOTH, partner).astype(F32)

    z_ring = [
        moves(n_row, n_col, lambda block, core, col: ((block + 2 * way) % n_block, core, col)) for way in (1, -1)
    ]
    x_ring = [
        moves(n_row, n_col, lambda block, core, col: (block, core, col // ring * ring + (col + way) % ring))
        for way in (1, -1)
    ]
    y_near = moves(n_row, n_col, lambda block, core, col: (block ^ 1, core, col))
    y_far = moves(n_row, n_col, lambda block, core, col: (block, core, col ^ ring))

    slots = jnp.arange(n_block)
    owner = slots ^ block
    z_ahead, y_other = (owner // 2 - block // 2) % 4, (owner ^ block) % 2
    here = jnp.concatenate((core[None], 2 * z_ahead + y_other))
    here_y = jnp.concatenate((core[None], 4 * y_other + z_ahead))
    there = jnp.concatenate((core[None], 2 * ((slots // 2 - col) % ring) + (slots ^ col // ring) % 2))

    turned_a = transposed(stripe, *cross_pair, there)
    step_t = start(turned_a, *x_ring)
    product_y = untransposed(after(swath, turned_a), *gram_y_pair, here)
    step_y = start(product_y, *z_ring)
    product_a = untransposed(after(swath, product_y), *cross_pair, here_y)
    product_a = product_a.reshape((2, 4) + product_a.shape[1:])
    step_t = join(step_t[0], *lax.optimization_barrier(step_t[1:] + (product_a,))[:2])
    step_y = join(step_y[0], *lax.optimization_barrier(step_y[1:] + (product_a,))[:2])
    product_x = untransposed(after(swath, step_t[1], step_y[1]), *gram_x_pair, here)
    step_x = start(product_x, *z_ring)
    total_t = finish(step_t, *x_ring)
    half_a = fold(product_a.astype(F32), y_near, BF16).astype(BF16)
    step_a = start(after(half_a, total_t), *z_ring)
    step_x = join(step_x[0], *lax.optimization_barrier(step_x[1:] + (total_t,))[:2])

    total_t = fold(total_t, y_far, BF16)
    from_gram_y = fold(finish(step_y, *z_ring), y_near, F32)
    from_gram_x = fold(after(finish(step_x, *z_ring), total_t), y_near, BF16)
    from_cross_t = finish(join(*step_a), *z_ring)
    from_cross_t = from_cross_t.reshape((-1,) + from_cross_t.shape[2:])
    pairs = moves(
        n_row, n_col, lambda block, core, col: ((2 * (col % ring) + col // ring) ^ block, core, block)
    )
    from_cross = lax.ppermute(total_t.astype(BF16), BOTH, pairs).astype(F32)

    shift_col = shifts[:, None, None]
    return (
        from_gram_y[None]
        - shift_col * (from_cross_t + from_cross)[None]
        + shift_col * shift_col * from_gram_x[None]
    )


def solution(mesh):
    def step(*args):
        return shards(mesh.shape["row"], mesh.shape["col"], *args)

    in_specs = (P("row", "col"), P("row", "col"), P("row", "col"), P(), P("row", "col"))
    out_specs = P(None, "row", "col")
    return jax.shard_map(step, mesh=mesh, in_specs=in_specs, out_specs=out_specs, check_vma=False)
```

```python
import jax
import jax.numpy as jnp
from jax import lax
from jax.experimental import pallas as pl
from jax.experimental.pallas import tpu as pltpu
from jax.sharding import PartitionSpec as P

BOTH = ("row", "col")
BF16 = jnp.bfloat16
F32 = jnp.float32
VMEM_BYTES = 48 * 2**20


def moves(n_row, n_col, target):
    pairs = []
    for block in range(n_row // 2):
        for core in range(2):
            for col in range(n_col):
                to_block, to_core, to_col = target(block, core, col)
                pairs.append(((2 * block + core) * n_col + col, (2 * to_block + to_core) * n_col + to_col))
    return pairs


def after(array, *others):
    return lax.optimization_barrier((array,) + others)[0]


def call(body, place, grid, in_specs, out_spec, out_shape, scratch, flops, *args):
    return pl.pallas_call(
        body,
        grid_spec=pltpu.PrefetchScalarGridSpec(
            num_scalar_prefetch=1, grid=grid, in_specs=in_specs, out_specs=out_spec, scratch_shapes=scratch
        ),
        out_shape=out_shape,
        compiler_params=pltpu.CompilerParams(vmem_limit_bytes=VMEM_BYTES),
        cost_estimate=pl.CostEstimate(
            flops=flops,
            bytes_accessed=sum(a.size * a.dtype.itemsize for a in args) + out_shape.size * 2,
            transcendentals=0,
        ),
    )(place, *args)


def untransposed(part, mine, other, place):
    slots, modes, depth = part.shape
    half, width = mine.shape
    block = 512

    def body(place, part, mine, other, out, tile):
        tile[pl.ds(pl.multiple_of(place[0] * half, half), half)] = mine[...].astype(BF16)
        tile[pl.ds(pl.multiple_of((1 - place[0]) * half, half), half)] = other[...].astype(BF16)
        rows = part[...].reshape(slots * modes, depth)
        total = jnp.dot(rows, tile[...], preferred_element_type=F32).astype(BF16)
        for slot in range(slots):
            out[place[1 + slot]] = total[slot * modes : (slot + 1) * modes]

    return call(
        body,
        place,
        (width // block,),
        [
            pl.BlockSpec((slots, modes, depth), lambda n, place: (0, 0, 0)),
            pl.BlockSpec((half, block), lambda n, place: (0, n)),
            pl.BlockSpec((half, block), lambda n, place: (0, n)),
        ],
        pl.BlockSpec((slots, modes, block), lambda n, place: (0, 0, n)),
        jax.ShapeDtypeStruct((slots, modes, width), BF16),
        [pltpu.VMEM((2 * half, block), BF16)],
        2 * slots * modes * depth * width,
        part,
        mine,
        other,
    )


def transposed(part, mine, other, place):
    slots, modes, depth = part.shape
    half = mine.shape[0]
    block = 512
    blocks = half // block

    def body(place, part, mine, other, out):
        own = pl.program_id(0) // blocks == place[0]
        tile = jnp.where(own, mine[...], other[...]).astype(BF16)
        rows = part[...].reshape(slots * modes, depth)
        total = lax.dot_general(rows, tile, (((1,), (1,)), ((), ())), preferred_element_type=F32)
        total = total.astype(BF16)
        for slot in range(slots):
            out[place[1 + slot]] = total[slot * modes : (slot + 1) * modes]

    return call(
        body,
        place,
        (2 * blocks,),
        [
            pl.BlockSpec((slots, modes, depth), lambda n, place: (0, 0, 0)),
            pl.BlockSpec((block, depth), lambda n, place: (n % blocks, 0)),
            pl.BlockSpec((block, depth), lambda n, place: (n % blocks, 0)),
        ],
        pl.BlockSpec((slots, modes, block), lambda n, place: (0, 0, n)),
        jax.ShapeDtypeStruct((slots, modes, 2 * half), BF16),
        [],
        4 * slots * modes * depth * half,
        part,
        mine,
        other,
    )


def shards(n_row, n_col, gram_x, cross, gram_y, shifts, modes):
    row, col = lax.axis_index("row"), lax.axis_index("col")
    core, block = row % 2, row // 2
    n_block = n_row // 2
    ring = n_col // 2
    swap_cores = moves(n_row, n_col, lambda block, core, col: (block, 1 - core, col))

    turned = lax.ppermute(
        modes, BOTH, moves(n_row, n_col, lambda block, core, col: (col, core, block ^ col))
    )
    pair = lax.ppermute(modes, BOTH, moves(n_row, n_col, lambda block, core, col: (block ^ 1, core, col)))
    gram_x_pair, cross_pair, gram_y_pair = [
        (tile, lax.ppermute(tile, BOTH, swap_cores)) for tile in (gram_x, cross, gram_y)
    ]
    pair = after(jnp.stack((modes, pair)), gram_x_pair, cross_pair, gram_y_pair)
    stripe = [pair]
    for step in range(2, n_block, 2):
        pairs = moves(n_row, n_col, lambda block, core, col: (block ^ step, core, col))
        stripe.append(lax.ppermute(pair, BOTH, pairs))

    copies = jnp.broadcast_to(after(turned, pair)[None], (n_col,) + turned.shape)
    swath = lax.all_to_all(copies, "col", split_axis=0, concat_axis=0, tiled=True)

    stripe = jnp.concatenate(stripe, axis=0)
    def start(product, ahead, back):
        parts = product.reshape((4, 2, -1) + product.shape[2:])
        return parts, lax.ppermute(parts[2, 0], BOTH, ahead), lax.ppermute(parts[2, 1], BOTH, back)

    def join(parts, came_ahead, came_back):
        def plus(part, came):
            return (part.astype(F32) + came.astype(F32)).astype(BF16)

        return (
            parts[0],
            jnp.stack((plus(parts[1, 0], came_ahead), parts[1, 1])),
            jnp.stack((parts[3, 0], plus(parts[3, 1], came_back))),
        )

    def finish(parts, ahead, back):
        mine, on, off = parts
        return (
            mine.astype(F32)
            + lax.ppermute(on, BOTH, ahead).astype(F32)
            + lax.ppermute(off, BOTH, back).astype(F32)
        )

    def ring_sum(parts, pairs):
        return parts[0].astype(F32) + sum(lax.ppermute(parts[i], BOTH, pairs[i]).astype(F32) for i in (1, 3, 2))

    def later(parts, *others):
        return lax.optimization_barrier(tuple(parts) + others)[: len(parts)]

    def fold(total, partner, dtype):
        return total[0] + lax.ppermute(total[1].astype(dtype), BOTH, partner).astype(F32)

    z_turns = [
        moves(n_row, n_col, lambda block, core, col: ((block + 2 * step) % n_block, core, col)) for step in range(4)
    ]
    z_ring = (z_turns[1], z_turns[3])
    x_ring = [
        moves(n_row, n_col, lambda block, core, col: (block, core, col // ring * ring + (col + way) % ring))
        for way in (1, -1)
    ]
    y_near = moves(n_row, n_col, lambda block, core, col: (block ^ 1, core, col))
    y_far = moves(n_row, n_col, lambda block, core, col: (block, core, col ^ ring))

    slots = jnp.arange(n_block)
    owner = slots ^ block
    z_ahead, y_other = (owner // 2 - block // 2) % 4, (owner ^ block) % 2
    here = jnp.concatenate((core[None], 2 * z_ahead + y_other))
    here_y = jnp.concatenate((core[None], 4 * y_other + z_ahead))
    there = jnp.concatenate((core[None], 2 * ((slots - col) % ring) + (slots // ring ^ col // ring)))

    turned_a = transposed(stripe, *cross_pair, there)
    step_t = start(turned_a, *x_ring)
    product_y = untransposed(after(swath, turned_a), *gram_y_pair, here)
    step_y = start(product_y, *z_ring)
    step_t = join(*later(step_t, product_y))
    product_a = untransposed(after(swath, step_t[1]), *cross_pair, here_y)
    product_a = product_a.reshape((2, 4) + product_a.shape[1:])
    product_x = untransposed(after(swath, product_a), *gram_x_pair, here)
    step_x = start(product_x, *z_ring)
    step_y = join(*later(step_y, product_x))
    total_t = after(finish(step_t, *x_ring), step_y[1])
    step_x = join(*later(step_x, total_t))
    half_a = after(fold(product_a, y_near, BF16).astype(BF16), step_x[1])

    total_t = after(fold(total_t, y_far, BF16), half_a)
    from_gram_y = fold(finish(step_y, *z_ring), y_near, BF16)
    from_gram_x = fold(after(finish(step_x, *z_ring), total_t), y_near, BF16)
    from_cross_t = ring_sum(half_a, z_turns)
    home = lax.ppermute(
        total_t.astype(BF16), BOTH, moves(n_row, n_col, lambda block, core, col: (block ^ col, core, col))
    )
    home = lax.ppermute(home, BOTH, moves(n_row, n_col, lambda block, core, col: (block, core, col ^ block)))
    from_cross = home.astype(F32)

    shift_col = shifts[:, None, None]
    return (
        from_gram_y[None]
        - shift_col * (from_cross_t + from_cross)[None]
        + shift_col * shift_col * from_gram_x[None]
    )


def solution(mesh):
    def step(*args):
        return shards(mesh.shape["row"], mesh.shape["col"], *args)

    in_specs = (P("row", "col"), P("row", "col"), P("row", "col"), P(), P("row", "col"))
    out_specs = P(None, "row", "col")
    return jax.shard_map(step, mesh=mesh, in_specs=in_specs, out_specs=out_specs, check_vma=False)
```

```python
import jax
import jax.numpy as jnp
from jax import lax
from jax.experimental import pallas as pl
from jax.experimental.pallas import tpu as pltpu
from jax.sharding import PartitionSpec as P

BOTH = ("row", "col")
BF16 = jnp.bfloat16
F32 = jnp.float32
VMEM_BYTES = 48 * 2**20


def moves(n_row, n_col, target):
    pairs = []
    for block in range(n_row // 2):
        for core in range(2):
            for col in range(n_col):
                to_block, to_core, to_col = target(block, core, col)
                pairs.append(((2 * block + core) * n_col + col, (2 * to_block + to_core) * n_col + to_col))
    return pairs


def after(array, *others):
    return lax.optimization_barrier((array,) + others)[0]


def call(body, place, grid, in_specs, out_spec, out_shape, scratch, flops, *args):
    return pl.pallas_call(
        body,
        grid_spec=pltpu.PrefetchScalarGridSpec(
            num_scalar_prefetch=1, grid=grid, in_specs=in_specs, out_specs=out_spec, scratch_shapes=scratch
        ),
        out_shape=out_shape,
        compiler_params=pltpu.CompilerParams(vmem_limit_bytes=VMEM_BYTES),
        cost_estimate=pl.CostEstimate(
            flops=flops,
            bytes_accessed=sum(a.size * a.dtype.itemsize for a in args) + out_shape.size * 2,
            transcendentals=0,
        ),
    )(place, *args)


def untransposed(part, mine, other, place):
    slots, modes, depth = part.shape
    half, width = mine.shape
    block = 512

    def body(place, part, mine, other, out, tile):
        tile[pl.ds(pl.multiple_of(place[0] * half, half), half)] = mine[...].astype(BF16)
        tile[pl.ds(pl.multiple_of((1 - place[0]) * half, half), half)] = other[...].astype(BF16)
        rows = part[...].reshape(slots * modes, depth)
        total = jnp.dot(rows, tile[...], preferred_element_type=F32).astype(BF16)
        for slot in range(slots):
            out[place[1 + slot]] = total[slot * modes : (slot + 1) * modes]

    return call(
        body,
        place,
        (width // block,),
        [
            pl.BlockSpec((slots, modes, depth), lambda n, place: (0, 0, 0)),
            pl.BlockSpec((half, block), lambda n, place: (0, n)),
            pl.BlockSpec((half, block), lambda n, place: (0, n)),
        ],
        pl.BlockSpec((slots, modes, block), lambda n, place: (0, 0, n)),
        jax.ShapeDtypeStruct((slots, modes, width), BF16),
        [pltpu.VMEM((2 * half, block), BF16)],
        2 * slots * modes * depth * width,
        part,
        mine,
        other,
    )


def transposed(part, mine, other, place):
    slots, modes, depth = part.shape
    half = mine.shape[0]
    block = 512
    blocks = half // block

    def body(place, part, mine, other, out):
        own = pl.program_id(0) // blocks == place[0]
        tile = jnp.where(own, mine[...], other[...]).astype(BF16)
        rows = part[...].reshape(slots * modes, depth)
        total = lax.dot_general(rows, tile, (((1,), (1,)), ((), ())), preferred_element_type=F32)
        total = total.astype(BF16)
        for slot in range(slots):
            out[place[1 + slot]] = total[slot * modes : (slot + 1) * modes]

    return call(
        body,
        place,
        (2 * blocks,),
        [
            pl.BlockSpec((slots, modes, depth), lambda n, place: (0, 0, 0)),
            pl.BlockSpec((block, depth), lambda n, place: (n % blocks, 0)),
            pl.BlockSpec((block, depth), lambda n, place: (n % blocks, 0)),
        ],
        pl.BlockSpec((slots, modes, block), lambda n, place: (0, 0, n)),
        jax.ShapeDtypeStruct((slots, modes, 2 * half), BF16),
        [],
        4 * slots * modes * depth * half,
        part,
        mine,
        other,
    )


def shards(n_row, n_col, gram_x, cross, gram_y, shifts, modes):
    row, col = lax.axis_index("row"), lax.axis_index("col")
    core, block = row % 2, row // 2
    n_block = n_row // 2
    ring = n_col // 2
    swap_cores = moves(n_row, n_col, lambda block, core, col: (block, 1 - core, col))

    turned = lax.ppermute(
        modes, BOTH, moves(n_row, n_col, lambda block, core, col: (col, core, block ^ col))
    )
    z_turns = [
        moves(n_row, n_col, lambda block, core, col: ((block + 2 * step) % n_block, core, col)) for step in range(4)
    ]
    z_ring = (z_turns[1], z_turns[3])
    pair = lax.ppermute(modes, BOTH, moves(n_row, n_col, lambda block, core, col: (block ^ 1, core, col)))
    gram_x_pair, cross_pair, gram_y_pair = [
        (tile, lax.ppermute(tile, BOTH, swap_cores)) for tile in (gram_x, cross, gram_y)
    ]
    pair = after(jnp.stack((modes, pair)), gram_x_pair, cross_pair, gram_y_pair)
    before, behind = lax.ppermute(pair, BOTH, z_ring[0]), lax.ppermute(pair, BOTH, z_ring[1])
    across = (lax.ppermute(before[:1], BOTH, z_ring[0]), lax.ppermute(behind[1:], BOTH, z_ring[1]))
    stripe = jnp.concatenate((pair, before, behind) + across, axis=0)

    copies = jnp.broadcast_to(after(turned, pair)[None], (n_col,) + turned.shape)
    swath = lax.all_to_all(copies, "col", split_axis=0, concat_axis=0, tiled=True)

    def start(product, ahead, back):
        parts = product.reshape((4, 2, -1) + product.shape[2:])
        return parts, lax.ppermute(parts[2, 0], BOTH, ahead), lax.ppermute(parts[2, 1], BOTH, back)

    def join(parts, came_ahead, came_back):
        def plus(part, came):
            return (part.astype(F32) + came.astype(F32)).astype(BF16)

        return (
            parts[0],
            jnp.stack((plus(parts[1, 0], came_ahead), parts[1, 1])),
            jnp.stack((parts[3, 0], plus(parts[3, 1], came_back))),
        )

    def finish(parts, ahead, back):
        mine, on, off = parts
        return (
            mine.astype(F32)
            + lax.ppermute(on, BOTH, ahead).astype(F32)
            + lax.ppermute(off, BOTH, back).astype(F32)
        )

    def ring_sum(parts, pairs):
        return parts[0].astype(F32) + sum(lax.ppermute(parts[i], BOTH, pairs[i]).astype(F32) for i in (1, 3, 2))

    def later(parts, *others):
        return lax.optimization_barrier(tuple(parts) + others)[: len(parts)]

    def fold(total, partner, dtype):
        return total[0] + lax.ppermute(total[1].astype(dtype), BOTH, partner).astype(F32)

    x_ring = [
        moves(n_row, n_col, lambda block, core, col: (block, core, col // ring * ring + (col + way) % ring))
        for way in (1, -1)
    ]
    y_near = moves(n_row, n_col, lambda block, core, col: (block ^ 1, core, col))
    y_far = moves(n_row, n_col, lambda block, core, col: (block, core, col ^ ring))

    slots = jnp.arange(n_block)
    owner = slots ^ block
    z_ahead, y_other = (owner // 2 - block // 2) % 4, (owner ^ block) % 2
    here = jnp.concatenate((core[None], 2 * z_ahead + y_other))
    here_y = jnp.concatenate((core[None], 4 * y_other + z_ahead))
    held = ((block + 2 * jnp.array((0, 0, -1, -1, 1, 1, 2, 2))) % n_block) ^ (slots % 2)
    summed = held ^ block
    there = jnp.concatenate((core[None], 2 * ((summed - col) % ring) + (summed // ring ^ col // ring)))

    turned_a = transposed(stripe, *cross_pair, there)
    step_t = start(turned_a, *x_ring)
    product_y = untransposed(after(swath, turned_a), *gram_y_pair, here)
    step_y = start(product_y, *z_ring)
    step_t = join(*later(step_t, product_y))
    product_a = untransposed(after(swath, step_t[1]), *cross_pair, here_y)
    product_a = product_a.reshape((2, 4) + product_a.shape[1:])
    product_x = untransposed(after(swath, product_a), *gram_x_pair, here)
    step_x = start(product_x, *z_ring)
    step_y = join(*later(step_y, product_x))
    total_t = after(finish(step_t, *x_ring), step_y[1])
    step_x = join(*later(step_x, total_t))
    half_a = after(fold(product_a, y_near, BF16).astype(BF16), step_x[1])

    total_t = after(fold(total_t, y_far, BF16), half_a)
    from_gram_y = fold(finish(step_y, *z_ring), y_near, BF16)
    from_gram_x = fold(after(finish(step_x, *z_ring), total_t), y_near, BF16)
    from_cross_t = ring_sum(half_a, z_turns)
    home = lax.ppermute(
        total_t.astype(BF16), BOTH, moves(n_row, n_col, lambda block, core, col: (block ^ col, core, col))
    )
    home = lax.ppermute(home, BOTH, moves(n_row, n_col, lambda block, core, col: (block, core, col ^ block)))
    from_cross = home.astype(F32)

    shift_col = shifts[:, None, None]
    return (
        from_gram_y[None]
        - shift_col * (from_cross_t + from_cross)[None]
        + shift_col * shift_col * from_gram_x[None]
    )


def solution(mesh):
    def step(*args):
        return shards(mesh.shape["row"], mesh.shape["col"], *args)

    in_specs = (P("row", "col"), P("row", "col"), P("row", "col"), P(), P("row", "col"))
    out_specs = P(None, "row", "col")
    return jax.shard_map(step, mesh=mesh, in_specs=in_specs, out_specs=out_specs, check_vma=False)
```

```python
import jax
import jax.numpy as jnp
from jax import lax
from jax.experimental import pallas as pl
from jax.experimental.pallas import tpu as pltpu
from jax.sharding import PartitionSpec as P

BOTH = ("row", "col")
BF16 = jnp.bfloat16
F32 = jnp.float32
VMEM_BYTES = 48 * 2**20


def moves(n_row, n_col, target):
    pairs = []
    for block in range(n_row // 2):
        for core in range(2):
            for col in range(n_col):
                to_block, to_core, to_col = target(block, core, col)
                pairs.append(((2 * block + core) * n_col + col, (2 * to_block + to_core) * n_col + to_col))
    return pairs


def after(array, *others):
    return lax.optimization_barrier((array,) + others)[0]


def call(body, place, grid, in_specs, out_spec, out_shape, scratch, flops, *args):
    return pl.pallas_call(
        body,
        grid_spec=pltpu.PrefetchScalarGridSpec(
            num_scalar_prefetch=1, grid=grid, in_specs=in_specs, out_specs=out_spec, scratch_shapes=scratch
        ),
        out_shape=out_shape,
        compiler_params=pltpu.CompilerParams(vmem_limit_bytes=VMEM_BYTES),
        cost_estimate=pl.CostEstimate(
            flops=flops,
            bytes_accessed=sum(a.size * a.dtype.itemsize for a in args) + out_shape.size * 2,
            transcendentals=0,
        ),
    )(place, *args)


def untransposed(part, mine, other, place):
    slots, modes, depth = part.shape
    half, width = mine.shape
    block = 512

    def body(place, part, mine, other, out, tile):
        tile[pl.ds(pl.multiple_of(place[0] * half, half), half)] = mine[...].astype(BF16)
        tile[pl.ds(pl.multiple_of((1 - place[0]) * half, half), half)] = other[...].astype(BF16)
        rows = part[...].reshape(slots * modes, depth)
        total = jnp.dot(rows, tile[...], preferred_element_type=F32).astype(BF16)
        for slot in range(slots):
            out[place[1 + slot]] = total[slot * modes : (slot + 1) * modes]

    return call(
        body,
        place,
        (width // block,),
        [
            pl.BlockSpec((slots, modes, depth), lambda n, place: (0, 0, 0)),
            pl.BlockSpec((half, block), lambda n, place: (0, n)),
            pl.BlockSpec((half, block), lambda n, place: (0, n)),
        ],
        pl.BlockSpec((slots, modes, block), lambda n, place: (0, 0, n)),
        jax.ShapeDtypeStruct((slots, modes, width), BF16),
        [pltpu.VMEM((2 * half, block), BF16)],
        2 * slots * modes * depth * width,
        part,
        mine,
        other,
    )


def transposed(part, mine, other, place):
    slots, modes, depth = part.shape
    half = mine.shape[0]
    block = 512
    blocks = half // block

    def body(place, part, mine, other, out):
        own = pl.program_id(0) // blocks == place[0]
        tile = jnp.where(own, mine[...], other[...]).astype(BF16)
        rows = part[...].reshape(slots * modes, depth)
        total = lax.dot_general(rows, tile, (((1,), (1,)), ((), ())), preferred_element_type=F32)
        total = total.astype(BF16)
        for slot in range(slots):
            out[place[1 + slot]] = total[slot * modes : (slot + 1) * modes]

    return call(
        body,
        place,
        (2 * blocks,),
        [
            pl.BlockSpec((slots, modes, depth), lambda n, place: (0, 0, 0)),
            pl.BlockSpec((block, depth), lambda n, place: (n % blocks, 0)),
            pl.BlockSpec((block, depth), lambda n, place: (n % blocks, 0)),
        ],
        pl.BlockSpec((slots, modes, block), lambda n, place: (0, 0, n)),
        jax.ShapeDtypeStruct((slots, modes, 2 * half), BF16),
        [],
        4 * slots * modes * depth * half,
        part,
        mine,
        other,
    )


def shards(n_row, n_col, gram_x, cross, gram_y, shifts, modes):
    row, col = lax.axis_index("row"), lax.axis_index("col")
    core, block = row % 2, row // 2
    n_block = n_row // 2
    ring = n_col // 2
    swap_cores = moves(n_row, n_col, lambda block, core, col: (block, 1 - core, col))

    turned = lax.ppermute(
        modes, BOTH, moves(n_row, n_col, lambda block, core, col: (col, core, block ^ col))
    )
    z_turns = [
        moves(n_row, n_col, lambda block, core, col: ((block + 2 * step) % n_block, core, col)) for step in range(4)
    ]
    z_ring = (z_turns[1], z_turns[3])
    pair = lax.ppermute(modes, BOTH, moves(n_row, n_col, lambda block, core, col: (block ^ 1, core, col)))
    gram_x_pair, cross_pair, gram_y_pair = [
        (tile, lax.ppermute(tile, BOTH, swap_cores)) for tile in (gram_x, cross, gram_y)
    ]
    pair = after(jnp.stack((modes, pair)), gram_x_pair, cross_pair, gram_y_pair)
    before, behind = lax.ppermute(pair, BOTH, z_ring[0]), lax.ppermute(pair, BOTH, z_ring[1])
    across = (lax.ppermute(before[:1], BOTH, z_ring[0]), lax.ppermute(behind[1:], BOTH, z_ring[1]))
    stripe = jnp.concatenate((pair, before, behind) + across, axis=0)

    copies = jnp.broadcast_to(after(turned, pair)[None], (n_col,) + turned.shape)
    swath = lax.all_to_all(copies, "col", split_axis=0, concat_axis=0, tiled=True)

    def start(product, ahead, back):
        parts = product.reshape((4, 2, -1) + product.shape[2:])
        return parts, lax.ppermute(parts[2, 0], BOTH, ahead), lax.ppermute(parts[2, 1], BOTH, back)

    def join(parts, came_ahead, came_back):
        def plus(part, came):
            return (part.astype(F32) + came.astype(F32)).astype(BF16)

        return (
            parts[0],
            jnp.stack((plus(parts[1, 0], came_ahead), parts[1, 1])),
            jnp.stack((parts[3, 0], plus(parts[3, 1], came_back))),
        )

    def finish(parts, ahead, back):
        mine, on, off = parts
        return (
            mine.astype(F32)
            + lax.ppermute(on, BOTH, ahead).astype(F32)
            + lax.ppermute(off, BOTH, back).astype(F32)
        )

    def ring_sum(parts, pairs):
        return parts[0].astype(F32) + sum(lax.ppermute(parts[i], BOTH, pairs[i]).astype(F32) for i in (1, 3, 2))

    def later(parts, *others):
        return lax.optimization_barrier(tuple(parts) + others)[: len(parts)]

    def fold(total, partner, dtype):
        return total[0] + lax.ppermute(total[1].astype(dtype), BOTH, partner).astype(F32)

    x_ring = [
        moves(n_row, n_col, lambda block, core, col: (block, core, col // ring * ring + (col + way) % ring))
        for way in (1, -1)
    ]
    y_near = moves(n_row, n_col, lambda block, core, col: (block ^ 1, core, col))
    y_far = moves(n_row, n_col, lambda block, core, col: (block, core, col ^ ring))

    slots = jnp.arange(n_block)
    owner = slots ^ block
    z_ahead, y_other = (owner // 2 - block // 2) % 4, (owner ^ block) % 2
    here = jnp.concatenate((core[None], 2 * z_ahead + y_other))
    here_y = jnp.concatenate((core[None], 4 * y_other + z_ahead))
    held = ((block + 2 * jnp.array((0, 0, -1, -1, 1, 1, 2, 2))) % n_block) ^ (slots % 2)
    summed = held ^ block
    there = jnp.concatenate((core[None], 2 * ((summed - col) % ring) + (summed // ring ^ col // ring)))

    turned_a = transposed(stripe, *cross_pair, there)
    step_t = start(turned_a, *x_ring)
    product_y = untransposed(after(swath, turned_a), *gram_y_pair, here)
    step_y = start(product_y, *z_ring)
    step_t = join(*later(step_t, product_y))
    product_a = untransposed(after(swath, step_t[1]), *cross_pair, here_y)
    product_a = product_a.reshape((2, 4) + product_a.shape[1:])
    step_y = join(*later(step_y, product_a))
    product_x = untransposed(after(swath, product_a, step_y[1]), *gram_x_pair, here)
    step_x = start(product_x, *z_ring)
    total_t = after(finish(step_t, *x_ring), step_y[1])
    step_x = join(*later(step_x, total_t))
    half_a = after(fold(product_a, y_near, BF16).astype(BF16), step_x[1])

    total_t = after(fold(total_t, y_far, BF16), half_a)
    from_gram_y = fold(finish(step_y, *z_ring), y_near, BF16)
    from_gram_x = fold(after(finish(step_x, *z_ring), total_t), y_near, BF16)
    home = lax.ppermute(
        total_t.astype(BF16), BOTH, moves(n_row, n_col, lambda block, core, col: (block ^ col, core, col))
    )
    from_cross_t = ring_sum(after(half_a, home), z_turns)
    home = lax.ppermute(home, BOTH, moves(n_row, n_col, lambda block, core, col: (block, core, col ^ block)))
    from_cross = home.astype(F32)

    shift_col = shifts[:, None, None]
    return (
        from_gram_y[None]
        - shift_col * (from_cross_t + from_cross)[None]
        + shift_col * shift_col * from_gram_x[None]
    )


def solution(mesh):
    def step(*args):
        return shards(mesh.shape["row"], mesh.shape["col"], *args)

    in_specs = (P("row", "col"), P("row", "col"), P("row", "col"), P(), P("row", "col"))
    out_specs = P(None, "row", "col")
    return jax.shard_map(step, mesh=mesh, in_specs=in_specs, out_specs=out_specs, check_vma=False)
```

```python
import jax
import jax.numpy as jnp
from jax import lax
from jax.experimental import pallas as pl
from jax.experimental.pallas import tpu as pltpu
from jax.sharding import PartitionSpec as P

BOTH = ("row", "col")
BF16 = jnp.bfloat16
F32 = jnp.float32
VMEM_BYTES = 48 * 2**20


def moves(n_row, n_col, target):
    pairs = []
    for block in range(n_row // 2):
        for core in range(2):
            for col in range(n_col):
                to_block, to_core, to_col = target(block, core, col)
                pairs.append(((2 * block + core) * n_col + col, (2 * to_block + to_core) * n_col + to_col))
    return pairs


def after(array, *others):
    return lax.optimization_barrier((array,) + others)[0]


def call(body, place, grid, in_specs, out_spec, out_shape, scratch, flops, *args):
    return pl.pallas_call(
        body,
        grid_spec=pltpu.PrefetchScalarGridSpec(
            num_scalar_prefetch=1, grid=grid, in_specs=in_specs, out_specs=out_spec, scratch_shapes=scratch
        ),
        out_shape=out_shape,
        compiler_params=pltpu.CompilerParams(vmem_limit_bytes=VMEM_BYTES),
        cost_estimate=pl.CostEstimate(
            flops=flops,
            bytes_accessed=sum(a.size * a.dtype.itemsize for a in args) + out_shape.size * 2,
            transcendentals=0,
        ),
    )(place, *args)


def untransposed(part, mine, other, place):
    slots, modes, depth = part.shape
    half, width = mine.shape
    block = 512

    def body(place, part, mine, other, out, tile):
        tile[pl.ds(pl.multiple_of(place[0] * half, half), half)] = mine[...].astype(BF16)
        tile[pl.ds(pl.multiple_of((1 - place[0]) * half, half), half)] = other[...].astype(BF16)
        rows = part[...].reshape(slots * modes, depth)
        total = jnp.dot(rows, tile[...], preferred_element_type=F32).astype(BF16)
        for slot in range(slots):
            out[place[1 + slot]] = total[slot * modes : (slot + 1) * modes]

    return call(
        body,
        place,
        (width // block,),
        [
            pl.BlockSpec((slots, modes, depth), lambda n, place: (0, 0, 0)),
            pl.BlockSpec((half, block), lambda n, place: (0, n)),
            pl.BlockSpec((half, block), lambda n, place: (0, n)),
        ],
        pl.BlockSpec((slots, modes, block), lambda n, place: (0, 0, n)),
        jax.ShapeDtypeStruct((slots, modes, width), BF16),
        [pltpu.VMEM((2 * half, block), BF16)],
        2 * slots * modes * depth * width,
        part,
        mine,
        other,
    )


def transposed(part, mine, other, place):
    slots, modes, depth = part.shape
    half = mine.shape[0]
    block = 512
    blocks = half // block

    def body(place, part, mine, other, out):
        own = pl.program_id(0) // blocks == place[0]
        tile = jnp.where(own, mine[...], other[...]).astype(BF16)
        rows = part[...].reshape(slots * modes, depth)
        total = lax.dot_general(rows, tile, (((1,), (1,)), ((), ())), preferred_element_type=F32)
        total = total.astype(BF16)
        for slot in range(slots):
            out[place[1 + slot]] = total[slot * modes : (slot + 1) * modes]

    return call(
        body,
        place,
        (2 * blocks,),
        [
            pl.BlockSpec((slots, modes, depth), lambda n, place: (0, 0, 0)),
            pl.BlockSpec((block, depth), lambda n, place: (n % blocks, 0)),
            pl.BlockSpec((block, depth), lambda n, place: (n % blocks, 0)),
        ],
        pl.BlockSpec((slots, modes, block), lambda n, place: (0, 0, n)),
        jax.ShapeDtypeStruct((slots, modes, 2 * half), BF16),
        [],
        4 * slots * modes * depth * half,
        part,
        mine,
        other,
    )


def shards(n_row, n_col, gram_x, cross, gram_y, shifts, modes):
    row, col = lax.axis_index("row"), lax.axis_index("col")
    core, block = row % 2, row // 2
    n_block = n_row // 2
    ring = n_col // 2
    swap_cores = moves(n_row, n_col, lambda block, core, col: (block, 1 - core, col))

    turned = lax.ppermute(
        modes, BOTH, moves(n_row, n_col, lambda block, core, col: (col, core, block ^ col))
    )
    z_turns = [
        moves(n_row, n_col, lambda block, core, col: ((block + 2 * step) % n_block, core, col)) for step in range(4)
    ]
    z_ring = (z_turns[1], z_turns[3])
    pair = lax.ppermute(modes, BOTH, moves(n_row, n_col, lambda block, core, col: (block ^ 1, core, col)))
    gram_x_pair, cross_pair, gram_y_pair = [
        (tile, lax.ppermute(tile, BOTH, swap_cores)) for tile in (gram_x, cross, gram_y)
    ]
    pair = after(jnp.stack((modes, pair)), gram_x_pair, cross_pair, gram_y_pair)
    before, behind = lax.ppermute(pair, BOTH, z_ring[0]), lax.ppermute(pair, BOTH, z_ring[1])
    across = (lax.ppermute(before[:1], BOTH, z_ring[0]), lax.ppermute(behind[1:], BOTH, z_ring[1]))
    stripe = jnp.concatenate((pair, before, behind) + across, axis=0)

    copies = jnp.broadcast_to(after(turned, pair)[None], (n_col,) + turned.shape)
    swath = lax.all_to_all(copies, "col", split_axis=0, concat_axis=0, tiled=True)

    def start(product, ahead, back):
        parts = product.reshape((4, 2, -1) + product.shape[2:])
        return parts, lax.ppermute(parts[2, 0], BOTH, ahead), lax.ppermute(parts[2, 1], BOTH, back)

    def join(parts, came_ahead, came_back):
        def plus(part, came):
            return (part.astype(F32) + came.astype(F32)).astype(BF16)

        return (
            parts[0],
            jnp.stack((plus(parts[1, 0], came_ahead), parts[1, 1])),
            jnp.stack((parts[3, 0], plus(parts[3, 1], came_back))),
        )

    def finish(parts, ahead, back):
        mine, on, off = parts
        return (
            mine.astype(F32)
            + lax.ppermute(on, BOTH, ahead).astype(F32)
            + lax.ppermute(off, BOTH, back).astype(F32)
        )

    def ring_sum(parts, pairs):
        return parts[0].astype(F32) + sum(lax.ppermute(parts[i], BOTH, pairs[i]).astype(F32) for i in (2, 1, 3))

    def later(parts, *others):
        return lax.optimization_barrier(tuple(parts) + others)[: len(parts)]

    def fold(total, partner, dtype):
        return total[0] + lax.ppermute(total[1].astype(dtype), BOTH, partner).astype(F32)

    x_ring = [
        moves(n_row, n_col, lambda block, core, col: (block, core, col // ring * ring + (col + way) % ring))
        for way in (1, -1)
    ]
    y_near = moves(n_row, n_col, lambda block, core, col: (block ^ 1, core, col))
    y_far = moves(n_row, n_col, lambda block, core, col: (block, core, col ^ ring))

    slots = jnp.arange(n_block)
    owner = slots ^ block
    z_ahead, y_other = (owner // 2 - block // 2) % 4, (owner ^ block) % 2
    here = jnp.concatenate((core[None], 2 * z_ahead + y_other))
    here_y = jnp.concatenate((core[None], 4 * y_other + z_ahead))
    held = ((block + 2 * jnp.array((0, 0, -1, -1, 1, 1, 2, 2))) % n_block) ^ (slots % 2)
    summed = held ^ block
    there = jnp.concatenate((core[None], 2 * ((summed - col) % ring) + (summed // ring ^ col // ring)))

    turned_a = transposed(stripe, *cross_pair, there)
    step_t = start(turned_a, *x_ring)
    product_y = untransposed(after(swath, turned_a), *gram_y_pair, here)
    step_y = start(product_y, *z_ring)
    step_t = join(*later(step_t, product_y))
    product_a = untransposed(after(swath, step_t[1]), *cross_pair, here_y)
    product_a = product_a.reshape((2, 4) + product_a.shape[1:])
    step_y = join(*later(step_y, product_a))
    product_x = untransposed(after(swath, product_a, step_y[1]), *gram_x_pair, here)
    step_x = start(product_x, *z_ring)
    total_t = after(finish(step_t, *x_ring), step_y[1])
    step_x = join(*later(step_x, total_t))
    half_a = after(fold(product_a, y_near, BF16).astype(BF16), step_x[1])

    total_t = after(fold(total_t, y_far, BF16), half_a)
    from_gram_y = fold(finish(step_y, *z_ring), y_near, BF16)
    from_gram_x = fold(after(finish(step_x, *z_ring), total_t), y_near, BF16)
    home = lax.ppermute(
        total_t.astype(BF16), BOTH, moves(n_row, n_col, lambda block, core, col: (block ^ col, core, col))
    )
    from_cross_t = ring_sum(after(half_a, home), z_turns)
    home = lax.ppermute(home, BOTH, moves(n_row, n_col, lambda block, core, col: (block, core, col ^ block)))
    from_cross = home.astype(F32)

    shift_col = shifts[:, None, None]
    return (
        from_gram_y[None]
        - shift_col * (from_cross_t + from_cross)[None]
        + shift_col * shift_col * from_gram_x[None]
    )


def solution(mesh):
    def step(*args):
        return shards(mesh.shape["row"], mesh.shape["col"], *args)

    in_specs = (P("row", "col"), P("row", "col"), P("row", "col"), P(), P("row", "col"))
    out_specs = P(None, "row", "col")
    return jax.shard_map(step, mesh=mesh, in_specs=in_specs, out_specs=out_specs, check_vma=False)
```
